32 devices in a mesh: patch: 8 (over z, x), lag: 4 (over y, core).
Axes of the slice: x: 2, y: 2, z: 4, core: 2. Of those that a mesh axis runs over, the one named last changes fastest.
Arguments:
- history: bfloat16 [4, 128, 8192], P('lag', None, 'patch'), may hold values from -6 to 6
- coupling: bfloat16 [4, 8192, 1024], P('lag', 'patch'), may hold values from -0.09375 to 0.09375
- inverse: bfloat16 [8192, 1024], P('patch'), may hold values from -0.1875 to 0.1875
- cotangent: bfloat16 [6, 128, 8192], P(None, 'lag', 'patch'), may hold values from -6 to 6
- targets: int32 [4, 8], P('lag'), may hold values from 0 to 7
Outputs:
- adjoint: bfloat16 [6, 128, 8192], P(None, 'lag', 'patch')
The draws below stay inside these ranges and needn't reach their ends.
Inputs may be any that keep to these rules, and one draw needn't show every extreme that they name: `targets`: each lag and source patch lists exactly one target patch; several sources may list the same target.
All inputs are finite; a program needn't handle non-finite values.
Results may differ from the reference program's by a relative error of at most 0.0085.
Values may be sent and summed in bfloat16 or wider, within the bound.
A program may use at most 64 MiB of HBM per device.

```python
import jax
import jax.numpy as jnp
from jax import lax

U = 1024
R = 128
STEPS = 6
LAGS = 4
PATCHES = 8


def set_ends(drawn, rng, smallest, high):
    index_at = [jax.random.randint(jax.random.fold_in(rng, axis), (), 0, length) for axis, length in enumerate(drawn.shape)]
    longest = drawn.shape.index(max(drawn.shape))
    neighbour = index_at[:longest] + [(index_at[longest] + 1) % drawn.shape[longest]] + index_at[longest + 1:]
    return drawn.at[tuple(index_at)].set(smallest).at[tuple(neighbour)].set(high)


def block_levels(stream_key, extent, cuts, low, largest):
    factor_of = 1.0
    for position, shards_of in cuts:
        steps = jax.random.uniform(jax.random.fold_in(jax.random.fold_in(stream_key, 6), position), (shards_of,), jnp.float32, low / len(cuts), largest / len(cuts))
        factor_of = factor_of * jnp.repeat(jnp.exp(steps), extent[position] // shards_of).reshape((-1,) + (1,) * (len(extent) - 1 - position))
    return factor_of


def gaussian(own_key, dims, width, bound, cuts=(), kind=jnp.bfloat16):
    entries = jax.random.normal(own_key, dims, jnp.float32) * width
    if len(cuts) > 0:
        entries = block_levels(own_key, dims, cuts, -0.22, 0.18) * entries
    return jnp.clip(entries, min=-bound, max=bound).astype(kind)


def setup_inputs(seed: int = 0) -> dict:
    key_of = jax.random.split(jax.random.key(seed), 6)
    history = gaussian(key_of[0], (LAGS, R, PATCHES * U), 1.0, 6.0, ((0, 4), (2, 8)))
    coupling = gaussian(key_of[1], (LAGS, PATCHES * U, U), (U * LAGS) ** -0.5, 0.09375, ((0, 4), (1, 8)))
    inverse = gaussian(key_of[2], (PATCHES * U, U), U ** -0.5, 0.1875, ((0, 8),))
    cotangent = gaussian(key_of[3], (STEPS, R, PATCHES * U), 1.0, 6.0, ((1, 4), (2, 8)))
    targets = set_ends(jax.random.randint(key_of[4], (LAGS, PATCHES), 0, PATCHES), jax.random.fold_in(key_of[4], 1), 0, PATCHES - 1).astype(jnp.int32)
    return dict(history=history, coupling=coupling, inverse=inverse, cotangent=cotangent, targets=targets)


def reference(history, coupling, inverse, cotangent, targets):
    coupling_tiles = coupling.reshape(LAGS, PATCHES, U, U)
    inverses = inverse.reshape(PATCHES, U, U).astype(jnp.float32)
    histories = history.reshape(LAGS, R, PATCHES, U)
    results = []
    for turn_index in range(STEPS):
        def one_lag(running, members):
            earlier, tile_block, target_row = members
            routed = jnp.take(earlier, target_row, axis=1).astype(jnp.float32)
            added = jnp.einsum("rpi,pij->rpj", routed, tile_block.astype(jnp.float32))
            return running + added, None

        start = jnp.zeros((R, PATCHES, U), jnp.float32)
        partial_value, _ = lax.scan(one_lag, start, (histories, coupling_tiles, targets))
        drive = cotangent[turn_index].reshape(R, PATCHES, U).astype(jnp.float32)
        residual = (drive - partial_value).astype(jnp.bfloat16)
        adjoint_now = jnp.einsum("rpi,pij->rpj", residual.astype(jnp.float32), inverses).astype(jnp.bfloat16)
        results.append(adjoint_now.reshape(R, PATCHES * U))
        histories = jnp.concatenate([adjoint_now[None], histories[:-1]], axis=0)
    return jnp.stack(results)
```

```python
import functools

import jax
import jax.numpy as jnp
from jax import lax
from jax.experimental import pallas as pl
from jax.experimental.pallas import tpu as pltpu
from jax.sharding import PartitionSpec as P

MESH = pl.DeviceIdType.MESH
LANES = 128


def kernel(
    patches, lags, steps, holders, width,
    history, coupling, inverse, cotangent, targets, out,
    held_start, staged_start, chosen, product, terms, states, held, current, staged, listed, listed_scalar,
    list_send, list_recv, list_local, start_send, start_recv, place_start_send, chosen_recv,
    term_send, term_recv, state_send, held_recv, place_send,
):
    patch = lax.axis_index("patch")
    lag = lax.axis_index("lag")
    rows = history.shape[1]
    unknowns = history.shape[2]
    depth = min(steps, lags)
    tile = min(unknowns, 256)

    def columns(index):
        return pl.ds(pl.multiple_of(index * width, LANES), width)

    def await_bytes(ref, semaphore):
        pltpu.make_async_copy(ref, ref, semaphore).wait()

    def send(src, dst, send_sem, recv_sem, to_patch, to_lag):
        pltpu.make_async_remote_copy(
            src_ref=src, dst_ref=dst, send_sem=send_sem, recv_sem=recv_sem,
            device_id=(to_patch, to_lag), device_id_type=MESH,
        ).start()

    barrier = pltpu.get_barrier_semaphore()
    own = patch * lags + lag

    @pl.loop(1, patches * lags)
    def _(offset):
        other = lax.rem(own + offset, patches * lags)
        pl.semaphore_signal(barrier, inc=1, device_id=(other // lags, lax.rem(other, lags)), device_id_type=MESH)

    pl.semaphore_wait(barrier, patches * lags - 1)

    @pl.loop(1, lags)
    def _(offset):
        to_lag = lax.rem(lag + offset, lags)
        send(targets, listed.at[lag], list_send, list_recv, patch, to_lag)

    @pl.loop(0, holders)
    def _(holder):
        @pl.when(holder != patch)
        def _():
            send(history.at[:, :, columns(holder)], held_start.at[patch], start_send, start_recv, holder, lag)

    listed[lag] = targets[...]

    @pl.when(patch < holders)
    def _():
        held_start[patch] = history[:, :, columns(patch)]

    await_bytes(listed.at[pl.ds(0, lags - 1)], list_recv)
    move = pltpu.make_async_copy(listed, listed_scalar, list_local)
    move.start()
    move.wait()

    @pl.when(patch < holders)
    def _():
        await_bytes(held_start.at[pl.ds(0, patches - 1)], start_recv)

        @pl.loop(0, depth)
        def _(step):
            to_lag = lag + step

            @pl.when(to_lag < lags)
            def _():
                @pl.loop(0, patches)
                def _(offset):
                    to_patch = lax.rem(patch + offset, patches)
                    staged_start[step, to_patch] = held_start[listed_scalar[to_lag, 0, to_patch]]
                    src = staged_start.at[step, to_patch]
                    dst = chosen.at[step, :, :, columns(patch)]
                    here = jnp.logical_and(step == 0, offset == 0)

                    @pl.when(here)
                    def _():
                        pltpu.make_async_copy(src, dst, chosen_recv.at[step]).start()

                    @pl.when(jnp.logical_not(here))
                    def _():
                        send(src, dst, place_start_send.at[step], chosen_recv.at[step], to_patch, to_lag)

    @pl.loop(0, steps)
    def _(step):
        await_bytes(chosen.at[step], chosen_recv.at[step])
        picked = chosen[step].reshape(lags * rows, unknowns)
        for first in range(0, unknowns, tile):
            part = jnp.dot(picked, coupling[0, :, first:first + tile], preferred_element_type=jnp.float32)
            product[step, :, :, first:first + tile] = part.astype(jnp.bfloat16).reshape(lags, rows, tile)

        @pl.loop(1, lags)
        def _(offset):
            to_lag = lax.rem(lag + offset, lags)
            send(product.at[step, to_lag], terms.at[step, lag], term_send.at[step], term_recv.at[step], patch, to_lag)

        total = cotangent[step].astype(jnp.float32) - product[step, lag].astype(jnp.float32)
        await_bytes(terms.at[step, pl.ds(0, lags - 1)], term_recv.at[step])
        for offset in range(1, lags):
            total = total - terms[step, lax.rem(lag + offset, lags)].astype(jnp.float32)
        residual = total.astype(jnp.bfloat16)
        for first in range(0, unknowns, tile):
            state = jnp.dot(residual, inverse[:, first:first + tile], preferred_element_type=jnp.float32)
            states[step, :, first:first + tile] = state.astype(jnp.bfloat16)
        out[step] = states[step]

        @pl.when(step + 1 < steps)
        def _():
            @pl.loop(0, holders)
            def _(holder):
                @pl.when(holder != patch)
                def _():
                    send(
                        states.at[step, :, columns(holder)], held.at[step, patch],
                        state_send.at[step], held_recv.at[step], holder, lag,
                    )

            @pl.when(patch < holders)
            def _():
                held[step, patch] = states[step, :, columns(patch)]
                await_bytes(held.at[step, pl.ds(0, patches - 1)], held_recv.at[step])
                current[...] = held[step]

                @pl.loop(0, lags)
                def _(to_lag):
                    later = step + 1 + to_lag

                    @pl.when(later < steps)
                    def _():
                        @pl.loop(0, patches)
                        def _(offset):
                            to_patch = lax.rem(patch + offset, patches)
                            staged[step, to_lag, to_patch] = current[listed_scalar[to_lag, 0, to_patch]]
                            src = staged.at[step, to_lag, to_patch]
                            dst = chosen.at[later, lag, :, columns(patch)]
                            here = jnp.logical_and(to_lag == lag, offset == 0)

                            @pl.when(here)
                            def _():
                                pltpu.make_async_copy(src, dst, chosen_recv.at[later]).start()

                            @pl.when(jnp.logical_not(here))
                            def _():
                                send(src, dst, place_send.at[step, to_lag], chosen_recv.at[later], to_patch, to_lag)

    await_bytes(listed.at[pl.ds(0, lags - 1)], list_send)

    def drained(ref, count_here, count_else, semaphore):
        @pl.when(patch < holders)
        def _():
            await_bytes(ref.at[pl.ds(0, count_here)], semaphore)

        if holders < patches:
            @pl.when(patch >= holders)
            def _():
                await_bytes(ref.at[pl.ds(0, count_else)], semaphore)

    drained(held_start, holders - 1, holders, start_send)

    @pl.when(patch < holders)
    def _():
        @pl.loop(0, depth)
        def _(step):
            @pl.when(lag + step < lags)
            def _():
                @pl.when(step == 0)
                def _():
                    await_bytes(staged_start.at[step, pl.ds(0, patches - 1)], place_start_send.at[step])

                @pl.when(step > 0)
                def _():
                    await_bytes(staged_start.at[step], place_start_send.at[step])

    @pl.loop(0, steps)
    def _(step):
        await_bytes(product.at[step, pl.ds(0, lags - 1)], term_send.at[step])

        @pl.when(step + 1 < steps)
        def _():
            drained(held.at[step], holders - 1, holders, state_send.at[step])

            @pl.when(patch < holders)
            def _():
                @pl.loop(0, lags)
                def _(to_lag):
                    @pl.when(step + 1 + to_lag < steps)
                    def _():
                        @pl.when(to_lag == lag)
                        def _():
                            await_bytes(staged.at[step, to_lag, pl.ds(0, patches - 1)], place_send.at[step, to_lag])

                        @pl.when(to_lag != lag)
                        def _():
                            await_bytes(staged.at[step, to_lag], place_send.at[step, to_lag])


def on_device(patches, lags, history, coupling, inverse, cotangent, targets):
    steps, rows, unknowns = cotangent.shape
    holders = min(patches, max(1, unknowns // LANES))
    width = unknowns // holders
    depth = min(steps, lags)
    vmem = pl.BlockSpec(memory_space=pltpu.VMEM)
    kind = history.dtype
    dma = pltpu.SemaphoreType.DMA
    return pl.pallas_call(
        functools.partial(kernel, patches, lags, steps, holders, width),
        out_shape=jax.ShapeDtypeStruct((steps, rows, unknowns), kind),
        in_specs=[vmem] * 5,
        out_specs=vmem,
        scratch_shapes=[
            pltpu.VMEM((patches, lags, rows, width), kind),
            pltpu.VMEM((depth, patches, lags, rows, width), kind),
            pltpu.VMEM((steps, lags, rows, unknowns), kind),
            pltpu.VMEM((steps, lags, rows, unknowns), kind),
            pltpu.VMEM((steps, lags, rows, unknowns), kind),
            pltpu.VMEM((steps, rows, unknowns), kind),
            pltpu.VMEM((steps, patches, rows, width), kind),
            pltpu.VMEM((patches, rows, width), kind),
            pltpu.VMEM((steps, lags, patches, rows, width), kind),
            pltpu.VMEM((lags, 1, patches), jnp.int32),
            pltpu.SMEM((lags, 1, patches), jnp.int32),
            dma, dma, dma, dma, dma, dma((depth,)), dma((steps,)),
            dma((steps,)), dma((steps,)), dma((steps,)), dma((steps,)), dma((steps, lags)),
        ],
        compiler_params=pltpu.CompilerParams(
            collective_id=0, has_side_effects=True, vmem_limit_bytes=48 * 1024 * 1024
        ),
    )(history.reshape(lags, rows, unknowns), coupling, inverse, cotangent, targets)


def solution(mesh):
    placed = (
        P("lag", None, "patch"),
        P("lag", "patch", None),
        P("patch", None),
        P(None, "lag", "patch"),
        P("lag", None),
    )
    return jax.shard_map(
        functools.partial(on_device, mesh.shape["patch"], mesh.shape["lag"]),
        mesh=mesh, in_specs=placed, out_specs=P(None, "lag", "patch"), check_vma=False,
    )
```

```python
import functools

import jax
import jax.numpy as jnp
from jax import lax
from jax.experimental import pallas as pl
from jax.experimental.pallas import tpu as pltpu
from jax.sharding import PartitionSpec as P

MESH = pl.DeviceIdType.MESH
LANES = 128


def kernel(
    patches, lags, steps, holders, width,
    history, coupling_far, inverse_far, cotangent_far, targets, out, coupling, inverse, cotangent,
    held_start, staged_start, chosen, product, terms, states, held, current, staged, listed, listed_scalar,
    list_send, list_recv, list_local, start_send, start_recv, place_start_send, chosen_recv,
    term_send, term_recv, state_send, held_recv, place_send, fetched, kept,
):
    patch = lax.axis_index("patch")
    lag = lax.axis_index("lag")
    rows = history.shape[1]
    unknowns = history.shape[2]
    depth = min(steps, lags)
    tile = max(width, min(unknowns, 256))

    def columns(index):
        return pl.ds(pl.multiple_of(index * width, LANES), width)

    def await_bytes(ref, semaphore):
        pltpu.make_async_copy(ref, ref, semaphore).wait()

    def send(src, dst, send_sem, recv_sem, to_patch, to_lag):
        pltpu.make_async_remote_copy(
            src_ref=src, dst_ref=dst, send_sem=send_sem, recv_sem=recv_sem,
            device_id=(to_patch, to_lag), device_id_type=MESH,
        ).start()

    fetches = [
        pltpu.make_async_copy(coupling_far.at[0], coupling, fetched.at[0]),
        pltpu.make_async_copy(inverse_far, inverse, fetched.at[1]),
        pltpu.make_async_copy(cotangent_far, cotangent, fetched.at[2]),
    ]
    for fetch in fetches:
        fetch.start()

    @pl.when(patch < holders)
    def _():
        pltpu.make_async_copy(history.at[:, :, columns(patch)], held_start.at[patch], kept).start()

    barrier = pltpu.get_barrier_semaphore()
    own = patch * lags + lag

    @pl.loop(1, patches * lags)
    def _(offset):
        other = lax.rem(own + offset, patches * lags)
        pl.semaphore_signal(barrier, inc=1, device_id=(other // lags, lax.rem(other, lags)), device_id_type=MESH)

    pl.semaphore_wait(barrier, patches * lags - 1)

    @pl.loop(1, lags)
    def _(offset):
        to_lag = lax.rem(lag + offset, lags)
        send(targets, listed.at[lag], list_send, list_recv, patch, to_lag)

    @pl.loop(0, holders)
    def _(holder):
        @pl.when(holder != patch)
        def _():
            send(history.at[:, :, columns(holder)], held_start.at[patch], start_send, start_recv, holder, lag)

    listed[lag] = targets[...]

    await_bytes(listed.at[pl.ds(0, lags - 1)], list_recv)
    move = pltpu.make_async_copy(listed, listed_scalar, list_local)
    move.start()
    move.wait()

    @pl.when(patch < holders)
    def _():
        await_bytes(held_start.at[patch], kept)
        await_bytes(held_start.at[pl.ds(0, patches - 1)], start_recv)

        @pl.loop(0, depth)
        def _(step):
            to_lag = lag + step

            @pl.when(to_lag < lags)
            def _():
                @pl.loop(0, patches)
                def _(offset):
                    to_patch = lax.rem(patch + offset, patches)
                    staged_start[step, to_patch] = held_start[listed_scalar[to_lag, 0, to_patch]]
                    src = staged_start.at[step, to_patch]
                    dst = chosen.at[step, patch]
                    here = jnp.logical_and(step == 0, offset == 0)

                    @pl.when(here)
                    def _():
                        pltpu.make_async_copy(src, dst, chosen_recv.at[step]).start()

                    @pl.when(jnp.logical_not(here))
                    def _():
                        send(src, dst, place_start_send.at[step], chosen_recv.at[step], to_patch, to_lag)

    for fetch in fetches:
        fetch.wait()

    @pl.loop(0, steps)
    def _(step):
        await_bytes(chosen.at[step], chosen_recv.at[step])
        picked = jnp.concatenate(
            [chosen[step, holder].reshape(lags * rows, width) for holder in range(holders)], axis=1
        )
        for first in range(0, unknowns, tile):
            part = jnp.dot(picked, coupling[:, first:first + tile], preferred_element_type=jnp.float32)
            product[step, :, :, first:first + tile] = part.astype(jnp.bfloat16).reshape(lags, rows, tile)

        @pl.loop(1, lags)
        def _(offset):
            to_lag = lax.rem(lag + offset, lags)
            send(product.at[step, to_lag], terms.at[step, lag], term_send.at[step], term_recv.at[step], patch, to_lag)

        total = cotangent[step].astype(jnp.float32) - product[step, lag].astype(jnp.float32)
        await_bytes(terms.at[step, pl.ds(0, lags - 1)], term_recv.at[step])
        for offset in range(1, lags):
            total = total - terms[step, lax.rem(lag + offset, lags)].astype(jnp.float32)
        residual = total.astype(jnp.bfloat16)
        for first in range(0, unknowns, tile):
            state = jnp.dot(residual, inverse[:, first:first + tile], preferred_element_type=jnp.float32)
            state = state.astype(jnp.bfloat16)
            out[step, :, first:first + tile] = state
            for part in range(0, tile, width):
                states[step, (first + part) // width] = state[:, part:part + width]

        @pl.when(step + 1 < steps)
        def _():
            @pl.loop(0, holders)
            def _(holder):
                @pl.when(holder != patch)
                def _():
                    send(
                        states.at[step, holder], held.at[step, patch],
                        state_send.at[step], held_recv.at[step], holder, lag,
                    )

            @pl.when(patch < holders)
            def _():
                held[step, patch] = states[step, patch]
                await_bytes(held.at[step, pl.ds(0, patches - 1)], held_recv.at[step])
                current[...] = held[step]

                @pl.loop(0, lags)
                def _(to_lag):
                    later = step + 1 + to_lag

                    @pl.when(later < steps)
                    def _():
                        @pl.loop(0, patches)
                        def _(offset):
                            to_patch = lax.rem(patch + offset, patches)
                            staged[step, to_lag, to_patch] = current[listed_scalar[to_lag, 0, to_patch]]
                            src = staged.at[step, to_lag, to_patch]
                            dst = chosen.at[later, patch, lag]
                            here = jnp.logical_and(to_lag == lag, offset == 0)

                            @pl.when(here)
                            def _():
                                pltpu.make_async_copy(src, dst, chosen_recv.at[later]).start()

                            @pl.when(jnp.logical_not(here))
                            def _():
                                send(src, dst, place_send.at[step, to_lag], chosen_recv.at[later], to_patch, to_lag)

    await_bytes(listed.at[pl.ds(0, lags - 1)], list_send)

    def drained(ref, count_here, count_else, semaphore):
        @pl.when(patch < holders)
        def _():
            await_bytes(ref.at[pl.ds(0, count_here)], semaphore)

        if holders < patches:
            @pl.when(patch >= holders)
            def _():
                await_bytes(ref.at[pl.ds(0, count_else)], semaphore)

    drained(held_start, holders - 1, holders, start_send)

    @pl.when(patch < holders)
    def _():
        @pl.loop(0, depth)
        def _(step):
            @pl.when(lag + step < lags)
            def _():
                @pl.when(step == 0)
                def _():
                    await_bytes(staged_start.at[step, pl.ds(0, patches - 1)], place_start_send.at[step])

                @pl.when(step > 0)
                def _():
                    await_bytes(staged_start.at[step], place_start_send.at[step])

    @pl.loop(0, steps)
    def _(step):
        await_bytes(product.at[step, pl.ds(0, lags - 1)], term_send.at[step])

        @pl.when(step + 1 < steps)
        def _():
            drained(held.at[step], holders - 1, holders, state_send.at[step])

            @pl.when(patch < holders)
            def _():
                @pl.loop(0, lags)
                def _(to_lag):
                    @pl.when(step + 1 + to_lag < steps)
                    def _():
                        @pl.when(to_lag == lag)
                        def _():
                            await_bytes(staged.at[step, to_lag, pl.ds(0, patches - 1)], place_send.at[step, to_lag])

                        @pl.when(to_lag != lag)
                        def _():
                            await_bytes(staged.at[step, to_lag], place_send.at[step, to_lag])


def on_device(patches, lags, history, coupling, inverse, cotangent, targets):
    steps, rows, unknowns = cotangent.shape
    holders = min(patches, max(1, unknowns // LANES))
    width = unknowns // holders
    depth = min(steps, lags)
    vmem = pl.BlockSpec(memory_space=pltpu.VMEM)
    far = pl.BlockSpec(memory_space=pl.ANY)
    kind = history.dtype
    dma = pltpu.SemaphoreType.DMA
    return pl.pallas_call(
        functools.partial(kernel, patches, lags, steps, holders, width),
        out_shape=jax.ShapeDtypeStruct((steps, rows, unknowns), kind),
        in_specs=[far] * 4 + [vmem],
        out_specs=vmem,
        scratch_shapes=[
            pltpu.VMEM(coupling.shape[1:], kind),
            pltpu.VMEM(inverse.shape, kind),
            pltpu.VMEM(cotangent.shape, kind),
            pltpu.VMEM((patches, lags, rows, width), kind),
            pltpu.VMEM((depth, patches, lags, rows, width), kind),
            pltpu.VMEM((steps, holders, lags, rows, width), kind),
            pltpu.VMEM((steps, lags, rows, unknowns), kind),
            pltpu.VMEM((steps, lags, rows, unknowns), kind),
            pltpu.VMEM((steps, holders, rows, width), kind),
            pltpu.VMEM((steps, patches, rows, width), kind),
            pltpu.VMEM((patches, rows, width), kind),
            pltpu.VMEM((steps, lags, patches, rows, width), kind),
            pltpu.VMEM((lags, 1, patches), jnp.int32),
            pltpu.SMEM((lags, 1, patches), jnp.int32),
            dma, dma, dma, dma, dma, dma((depth,)), dma((steps,)),
            dma((steps,)), dma((steps,)), dma((steps,)), dma((steps,)), dma((steps, lags)), dma((3,)), dma,
        ],
        compiler_params=pltpu.CompilerParams(
            collective_id=0, has_side_effects=True, vmem_limit_bytes=48 * 1024 * 1024
        ),
    )(history.reshape(lags, rows, unknowns), coupling, inverse, cotangent, targets)


def solution(mesh):
    placed = (
        P("lag", None, "patch"),
        P("lag", "patch", None),
        P("patch", None),
        P(None, "lag", "patch"),
        P("lag", None),
    )
    return jax.shard_map(
        functools.partial(on_device, mesh.shape["patch"], mesh.shape["lag"]),
        mesh=mesh, in_specs=placed, out_specs=P(None, "lag", "patch"), check_vma=False,
    )
```

```python
import functools

import jax
import jax.numpy as jnp
from jax import lax
from jax.experimental import pallas as pl
from jax.experimental.pallas import tpu as pltpu
from jax.sharding import PartitionSpec as P

MESH = pl.DeviceIdType.MESH
LANES = 128


def kernel(
    patches, lags, steps, holders, width, span,
    history, coupling_far, inverse_far, cotangent_far, targets, out, coupling, inverse, cotangent,
    held_start, staged_start, chosen, product, residual, terms, states, held, current, staged, listed, listed_scalar,
    list_send, list_recv, list_local, start_send, start_recv, place_start_send, chosen_recv,
    term_send, term_recv, state_send, held_recv, place_send, fetched, kept, out_send, out_recv,
):
    patch = lax.axis_index("patch")
    lag = lax.axis_index("lag")
    groups, group_rows = chosen.shape[2:4]
    unknowns = history.shape[2]
    rows = out.shape[1]
    holds = jnp.logical_and(lax.rem(lag, span) == span - 1, patch < holders)
    depth = min(steps, lags)
    tile = max(width, min(unknowns, 256))

    def columns(index):
        return pl.ds(pl.multiple_of(index * width, LANES), width)

    def await_bytes(ref, semaphore):
        pltpu.make_async_copy(ref, ref, semaphore).wait()

    def send(src, dst, send_sem, recv_sem, to_patch, to_lag):
        pltpu.make_async_remote_copy(
            src_ref=src, dst_ref=dst, send_sem=send_sem, recv_sem=recv_sem,
            device_id=(to_patch, to_lag), device_id_type=MESH,
        ).start()

    fetches = [
        pltpu.make_async_copy(coupling_far.at[0], coupling, fetched.at[0]),
        pltpu.make_async_copy(inverse_far, inverse, fetched.at[1]),
        pltpu.make_async_copy(cotangent_far, cotangent, fetched.at[2]),
    ]
    for fetch in fetches:
        fetch.start()

    @pl.when(patch < holders)
    def _():
        pltpu.make_async_copy(history.at[:, :, columns(patch)], held_start.at[patch], kept).start()

    barrier = pltpu.get_barrier_semaphore()
    own = patch * lags + lag

    @pl.loop(1, patches * lags)
    def _(offset):
        other = lax.rem(own + offset, patches * lags)
        pl.semaphore_signal(barrier, inc=1, device_id=(other // lags, lax.rem(other, lags)), device_id_type=MESH)

    pl.semaphore_wait(barrier, patches * lags - 1)

    @pl.loop(1, lags)
    def _(offset):
        to_lag = lax.rem(lag + offset, lags)
        send(targets, listed.at[lag], list_send, list_recv, patch, to_lag)

    @pl.loop(0, holders)
    def _(holder):
        @pl.when(holder != patch)
        def _():
            send(history.at[:, :, columns(holder)], held_start.at[patch], start_send, start_recv, holder, lag)

    listed[lag] = targets[...]

    await_bytes(listed.at[pl.ds(0, lags - 1)], list_recv)
    move = pltpu.make_async_copy(listed, listed_scalar, list_local)
    move.start()
    move.wait()

    @pl.when(patch < holders)
    def _():
        await_bytes(held_start.at[patch], kept)
        await_bytes(held_start.at[pl.ds(0, patches - 1)], start_recv)

        @pl.loop(0, depth)
        def _(step):
            to_lag = lag + step

            @pl.when(to_lag < lags)
            def _():
                @pl.loop(0, patches)
                def _(offset):
                    to_patch = lax.rem(patch + offset, patches)
                    staged_start[step, to_patch] = held_start[listed_scalar[to_lag, 0, to_patch]]
                    src = staged_start.at[step, to_patch]
                    dst = chosen.at[step, patch]
                    here = jnp.logical_and(step == 0, offset == 0)

                    @pl.when(here)
                    def _():
                        pltpu.make_async_copy(src, dst, chosen_recv.at[step]).start()

                    @pl.when(jnp.logical_not(here))
                    def _():
                        send(src, dst, place_start_send.at[step], chosen_recv.at[step], to_patch, to_lag)

    for fetch in fetches:
        fetch.wait()

    @pl.loop(0, steps)
    def _(step):
        await_bytes(chosen.at[step], chosen_recv.at[step])
        picked = jnp.concatenate(
            [chosen[step, holder].reshape(groups * group_rows, width) for holder in range(holders)], axis=1
        )

        def driven(first):
            part = jnp.dot(picked, coupling[:, first:first + tile], preferred_element_type=jnp.float32)
            drive = cotangent[step, :, first:first + tile].astype(jnp.float32)
            blocks = part.reshape(lags, rows, tile)
            return [jnp.where(lag == block, drive, 0.0) - blocks[block] for block in range(lags)]

        @pl.when(lag > 0)
        def _():
            for first in range(0, unknowns, tile):
                for block, value in enumerate(driven(first)):
                    product[step, block, :, first:first + tile] = value.astype(jnp.bfloat16)
            send(product.at[step], terms.at[step, lag - 1], term_send.at[step], term_recv.at[step], patch, 0)

        @pl.when(lag == 0)
        def _():
            await_bytes(terms.at[step], term_recv.at[step])
            for first in range(0, unknowns, tile):
                for block, value in enumerate(driven(first)):
                    for other in range(lags - 1):
                        value = value + terms[step, other, block, :, first:first + tile].astype(jnp.float32)
                    residual[block, :, first:first + tile] = value.astype(jnp.bfloat16)
            drive = residual[...].reshape(lags * rows, unknowns)
            for first in range(0, unknowns, tile):
                state = jnp.dot(drive, inverse[:, first:first + tile], preferred_element_type=jnp.float32)
                state = state.astype(jnp.bfloat16)
                product[step, :, :, first:first + tile] = state.reshape(lags, rows, tile)
                for part in range(0, tile, width):
                    holder = (first + part) // width
                    states[step, holder] = state[:, part:part + width].reshape(groups, group_rows, width)

                    @pl.when(step + 1 < steps)
                    def _():
                        for group in range(groups):
                            send(
                                states.at[step, holder, group], held.at[step, patch],
                                state_send.at[step], held_recv.at[step], holder, group * span + span - 1,
                            )
            out[step] = product[step, 0]

            @pl.loop(1, lags)
            def _(block):
                send(product.at[step, block], out.at[step], out_send, out_recv, patch, block)

        @pl.when(jnp.logical_and(step > 0, holds))
        def _():
            done = step - 1
            await_bytes(held.at[done], held_recv.at[done])
            current[...] = held[done]

            @pl.loop(0, min(lags, steps - 1))
            def _(to_lag):
                later = step + to_lag

                @pl.when(later < steps)
                def _():
                    @pl.loop(0, patches)
                    def _(offset):
                        to_patch = lax.rem(patch + offset, patches)
                        staged[done, to_lag, to_patch] = current[listed_scalar[to_lag, 0, to_patch]]
                        src = staged.at[done, to_lag, to_patch]
                        dst = chosen.at[later, patch, lag // span]
                        here = jnp.logical_and(to_lag == lag, offset == 0)

                        @pl.when(here)
                        def _():
                            pltpu.make_async_copy(src, dst, chosen_recv.at[later]).start()

                        @pl.when(jnp.logical_not(here))
                        def _():
                            send(src, dst, place_send.at[done, to_lag], chosen_recv.at[later], to_patch, to_lag)

    await_bytes(listed.at[pl.ds(0, lags - 1)], list_send)

    @pl.when(patch < holders)
    def _():
        await_bytes(held_start.at[pl.ds(0, holders - 1)], start_send)

        @pl.loop(0, depth)
        def _(step):
            @pl.when(lag + step < lags)
            def _():
                @pl.when(step == 0)
                def _():
                    await_bytes(staged_start.at[step, pl.ds(0, patches - 1)], place_start_send.at[step])

                @pl.when(step > 0)
                def _():
                    await_bytes(staged_start.at[step], place_start_send.at[step])

    if holders < patches:
        @pl.when(patch >= holders)
        def _():
            await_bytes(held_start.at[pl.ds(0, holders)], start_send)

    @pl.when(lag == 0)
    def _():
        await_bytes(product.at[:, pl.ds(0, lags - 1)], out_send)

    @pl.when(lag > 0)
    def _():
        await_bytes(out, out_recv)

    @pl.loop(0, steps)
    def _(step):
        @pl.when(lag > 0)
        def _():
            await_bytes(product.at[step], term_send.at[step])

        @pl.when(jnp.logical_and(step + 1 < steps, lag == 0))
        def _():
            await_bytes(states.at[step], state_send.at[step])

        @pl.when(jnp.logical_and(step + 1 < steps, holds))
        def _():
            @pl.loop(0, min(lags, steps - 1))
            def _(to_lag):
                @pl.when(step + 1 + to_lag < steps)
                def _():
                    @pl.when(to_lag == lag)
                    def _():
                        await_bytes(staged.at[step, to_lag, pl.ds(0, patches - 1)], place_send.at[step, to_lag])

                    @pl.when(to_lag != lag)
                    def _():
                        await_bytes(staged.at[step, to_lag], place_send.at[step, to_lag])


def on_device(patches, lags, history, coupling, inverse, cotangent, targets):
    steps, rows, unknowns = cotangent.shape
    holders = min(patches, max(1, unknowns // LANES))
    width = unknowns // holders
    depth = min(steps, lags)
    span = 2
    groups, group_rows = lags // span, rows * span
    vmem = pl.BlockSpec(memory_space=pltpu.VMEM)
    far = pl.BlockSpec(memory_space=pl.ANY)
    kind = history.dtype
    dma = pltpu.SemaphoreType.DMA
    return pl.pallas_call(
        functools.partial(kernel, patches, lags, steps, holders, width, span),
        out_shape=jax.ShapeDtypeStruct((steps, rows, unknowns), kind),
        in_specs=[far] * 4 + [vmem],
        out_specs=vmem,
        scratch_shapes=[
            pltpu.VMEM(coupling.shape[1:], kind),
            pltpu.VMEM(inverse.shape, kind),
            pltpu.VMEM(cotangent.shape, kind),
            pltpu.VMEM((patches, groups, group_rows, width), kind),
            pltpu.VMEM((depth, patches, groups, group_rows, width), kind),
            pltpu.VMEM((steps, holders, groups, group_rows, width), kind),
            pltpu.VMEM((steps, lags, rows, unknowns), kind),
            pltpu.VMEM((lags, rows, unknowns), kind),
            pltpu.VMEM((steps, lags - 1, lags, rows, unknowns), kind),
            pltpu.VMEM((steps, holders, groups, group_rows, width), kind),
            pltpu.VMEM((steps, patches, group_rows, width), kind),
            pltpu.VMEM((patches, group_rows, width), kind),
            pltpu.VMEM((steps - 1, min(lags, steps - 1), patches, group_rows, width), kind),
            pltpu.VMEM((lags, 1, patches), jnp.int32),
            pltpu.SMEM((lags, 1, patches), jnp.int32),
            dma, dma, dma, dma, dma, dma((depth,)), dma((steps,)),
            dma((steps,)), dma((steps,)), dma((steps,)), dma((steps,)), dma((steps, lags)),
            dma((3,)), dma, dma, dma,
        ],
        compiler_params=pltpu.CompilerParams(
            collective_id=0, has_side_effects=True, vmem_limit_bytes=48 * 1024 * 1024
        ),
    )(history.reshape(groups, group_rows, unknowns), coupling, inverse, cotangent, targets)


def solution(mesh):
    placed = (
        P("lag", None, "patch"),
        P("lag", "patch", None),
        P("patch", None),
        P(None, "lag", "patch"),
        P("lag", None),
    )
    return jax.shard_map(
        functools.partial(on_device, mesh.shape["patch"], mesh.shape["lag"]),
        mesh=mesh, in_specs=placed, out_specs=P(None, "lag", "patch"), check_vma=False,
    )
```

```python
import functools

import jax
import jax.numpy as jnp
from jax import lax
from jax.experimental import pallas as pl
from jax.experimental.pallas import tpu as pltpu
from jax.sharding import PartitionSpec as P

MESH = pl.DeviceIdType.MESH
LANES = 128


def kernel(
    patches, lags, steps, holders, width, span,
    history, coupling_far, inverse_far, cotangent_far, targets, out, coupling, inverse, cotangent,
    held_start, staged_start, chosen, product, residual, terms, states, held, current, staged, listed, listed_scalar,
    list_send, list_recv, list_local, start_send, start_recv, place_start_send, chosen_recv,
    term_send, term_recv, state_send, held_recv, place_send, fetched, kept, out_send, out_recv,
):
    patch = lax.axis_index("patch")
    lag = lax.axis_index("lag")
    groups, group_rows = chosen.shape[2:4]
    unknowns = history.shape[2]
    rows = out.shape[1]
    holds = jnp.logical_and(lax.rem(lag, span) == span - 1, patch < holders)
    depth = min(steps, lags)
    tile = max(width, min(unknowns, 256))

    def columns(index):
        return pl.ds(pl.multiple_of(index * width, LANES), width)

    def await_bytes(ref, semaphore):
        pltpu.make_async_copy(ref, ref, semaphore).wait()

    def send(src, dst, send_sem, recv_sem, to_patch, to_lag):
        pltpu.make_async_remote_copy(
            src_ref=src, dst_ref=dst, send_sem=send_sem, recv_sem=recv_sem,
            device_id=(to_patch, to_lag), device_id_type=MESH,
        ).start()

    fetches = [
        pltpu.make_async_copy(coupling_far.at[0], coupling, fetched.at[0]),
        pltpu.make_async_copy(inverse_far, inverse, fetched.at[1]),
        pltpu.make_async_copy(cotangent_far, cotangent, fetched.at[2]),
    ]
    for fetch in fetches:
        fetch.start()

    @pl.when(patch < holders)
    def _():
        pltpu.make_async_copy(history.at[:, :, columns(patch)], held_start.at[patch], kept).start()

    barrier = pltpu.get_barrier_semaphore()
    own = patch * lags + lag

    @pl.loop(1, patches * lags)
    def _(offset):
        other = lax.rem(own + offset, patches * lags)
        pl.semaphore_signal(barrier, inc=1, device_id=(other // lags, lax.rem(other, lags)), device_id_type=MESH)

    pl.semaphore_wait(barrier, patches * lags - 1)

    @pl.loop(1, lags)
    def _(offset):
        to_lag = lax.rem(lag + offset, lags)
        send(targets, listed.at[lag], list_send, list_recv, patch, to_lag)

    @pl.loop(0, holders)
    def _(holder):
        @pl.when(holder != patch)
        def _():
            send(history.at[:, :, columns(holder)], held_start.at[patch], start_send, start_recv, holder, lag)

    listed[lag] = targets[...]

    await_bytes(listed.at[pl.ds(0, lags - 1)], list_recv)
    move = pltpu.make_async_copy(listed, listed_scalar, list_local)
    move.start()
    move.wait()

    @pl.when(patch < holders)
    def _():
        await_bytes(held_start.at[patch], kept)
        await_bytes(held_start.at[pl.ds(0, patches - 1)], start_recv)

        @pl.loop(0, depth)
        def _(step):
            to_lag = lag + step

            @pl.when(to_lag < lags)
            def _():
                @pl.loop(0, patches)
                def _(offset):
                    to_patch = lax.rem(patch + offset, patches)
                    staged_start[step, to_patch] = held_start[listed_scalar[to_lag, 0, to_patch]]
                    src = staged_start.at[step, to_patch]
                    dst = chosen.at[step, patch]
                    here = jnp.logical_and(step == 0, offset == 0)

                    @pl.when(here)
                    def _():
                        pltpu.make_async_copy(src, dst, chosen_recv.at[step]).start()

                    @pl.when(jnp.logical_not(here))
                    def _():
                        send(src, dst, place_start_send.at[step], chosen_recv.at[step], to_patch, to_lag)

    for fetch in fetches:
        fetch.wait()

    @pl.loop(0, steps)
    def _(step):
        await_bytes(chosen.at[step], chosen_recv.at[step])
        picked = jnp.concatenate(
            [chosen[step, holder].reshape(groups * group_rows, width) for holder in range(holders)], axis=1
        )

        def driven(first):
            part = jnp.dot(picked, coupling[:, first:first + tile], preferred_element_type=jnp.float32)
            drive = cotangent[step, :, first:first + tile].astype(jnp.float32)
            blocks = part.reshape(lags, rows, tile)
            return [jnp.where(lag == block, drive, 0.0) - blocks[block] for block in range(lags)]

        @pl.when(lag > 0)
        def _():
            for first in range(0, unknowns, tile):
                for block, value in enumerate(driven(first)):
                    product[step, block, :, first:first + tile] = value.astype(jnp.bfloat16)

            @pl.when(lax.rem(lag, span) == 1)
            def _():
                send(product.at[step], terms.at[step, 0], term_send.at[step], term_recv.at[step], patch, lag - 1)

            @pl.when(lax.rem(lag, span) == 0)
            def _():
                await_bytes(terms.at[step, 0], term_recv.at[step])
                both = product[step].astype(jnp.float32) + terms[step, 0].astype(jnp.float32)
                product[step] = both.astype(jnp.bfloat16)
                send(product.at[step], terms.at[step, lag // span], term_send.at[step], term_recv.at[step], patch, 0)

        @pl.when(lag == 0)
        def _():
            await_bytes(terms.at[step], term_recv.at[step])
            for first in range(0, unknowns, tile):
                for block, value in enumerate(driven(first)):
                    for other in range(groups):
                        value = value + terms[step, other, block, :, first:first + tile].astype(jnp.float32)
                    residual[block, :, first:first + tile] = value.astype(jnp.bfloat16)
            drive = residual[...].reshape(lags * rows, unknowns)
            for first in range(0, unknowns, tile):
                state = jnp.dot(drive, inverse[:, first:first + tile], preferred_element_type=jnp.float32)
                state = state.astype(jnp.bfloat16)
                product[step, :, :, first:first + tile] = state.reshape(lags, rows, tile)
                for part in range(0, tile, width):
                    holder = (first + part) // width
                    states[step, holder] = state[:, part:part + width].reshape(groups, group_rows, width)

            @pl.when(step + 1 < steps)
            def _():
                for offset in range(holders):
                    holder = lax.rem(patch + offset, holders)
                    for group in range(groups):
                        send(
                            states.at[step, holder, group], held.at[step, patch],
                            state_send.at[step], held_recv.at[step], holder, group * span + span - 1,
                        )

            out[step] = product[step, 0]

            @pl.loop(1, lags)
            def _(block):
                send(product.at[step, block], out.at[step], out_send, out_recv, patch, block)

        @pl.when(jnp.logical_and(step > 0, holds))
        def _():
            done = step - 1
            await_bytes(held.at[done], held_recv.at[done])
            current[...] = held[done]

            @pl.loop(0, min(lags, steps - 1))
            def _(to_lag):
                later = step + to_lag

                @pl.when(later < steps)
                def _():
                    @pl.loop(0, patches, unroll=True)
                    def _(to_patch):
                        staged[done, to_lag, to_patch] = current[listed_scalar[to_lag, 0, to_patch]]

                    @pl.loop(0, patches, unroll=True)
                    def _(offset):
                        to_patch = lax.rem(patch + offset, patches)
                        src = staged.at[done, to_lag, to_patch]
                        dst = chosen.at[later, patch, lag // span]
                        here = jnp.logical_and(to_lag == lag, offset == 0)

                        @pl.when(here)
                        def _():
                            pltpu.make_async_copy(src, dst, chosen_recv.at[later]).start()

                        @pl.when(jnp.logical_not(here))
                        def _():
                            send(src, dst, place_send.at[done, to_lag], chosen_recv.at[later], to_patch, to_lag)

    await_bytes(listed.at[pl.ds(0, lags - 1)], list_send)

    @pl.when(patch < holders)
    def _():
        await_bytes(held_start.at[pl.ds(0, holders - 1)], start_send)

        @pl.loop(0, depth)
        def _(step):
            @pl.when(lag + step < lags)
            def _():
                @pl.when(step == 0)
                def _():
                    await_bytes(staged_start.at[step, pl.ds(0, patches - 1)], place_start_send.at[step])

                @pl.when(step > 0)
                def _():
                    await_bytes(staged_start.at[step], place_start_send.at[step])

    if holders < patches:
        @pl.when(patch >= holders)
        def _():
            await_bytes(held_start.at[pl.ds(0, holders)], start_send)

    @pl.when(lag == 0)
    def _():
        await_bytes(product.at[:, pl.ds(0, lags - 1)], out_send)

    @pl.when(lag > 0)
    def _():
        await_bytes(out, out_recv)

    @pl.loop(0, steps)
    def _(step):
        @pl.when(lag > 0)
        def _():
            await_bytes(product.at[step], term_send.at[step])

        @pl.when(jnp.logical_and(step + 1 < steps, lag == 0))
        def _():
            await_bytes(states.at[step], state_send.at[step])

        @pl.when(jnp.logical_and(step + 1 < steps, holds))
        def _():
            @pl.loop(0, min(lags, steps - 1))
            def _(to_lag):
                @pl.when(step + 1 + to_lag < steps)
                def _():
                    @pl.when(to_lag == lag)
                    def _():
                        await_bytes(staged.at[step, to_lag, pl.ds(0, patches - 1)], place_send.at[step, to_lag])

                    @pl.when(to_lag != lag)
                    def _():
                        await_bytes(staged.at[step, to_lag], place_send.at[step, to_lag])


def on_device(patches, lags, history, coupling, inverse, cotangent, targets):
    steps, rows, unknowns = cotangent.shape
    holders = min(patches, max(1, unknowns // LANES))
    width = unknowns // holders
    depth = min(steps, lags)
    span = 2
    groups, group_rows = lags // span, rows * span
    vmem = pl.BlockSpec(memory_space=pltpu.VMEM)
    far = pl.BlockSpec(memory_space=pl.ANY)
    kind = history.dtype
    dma = pltpu.SemaphoreType.DMA
    return pl.pallas_call(
        functools.partial(kernel, patches, lags, steps, holders, width, span),
        out_shape=jax.ShapeDtypeStruct((steps, rows, unknowns), kind),
        in_specs=[far] * 4 + [vmem],
        out_specs=vmem,
        scratch_shapes=[
            pltpu.VMEM(coupling.shape[1:], kind),
            pltpu.VMEM(inverse.shape, kind),
            pltpu.VMEM(cotangent.shape, kind),
            pltpu.VMEM((patches, groups, group_rows, width), kind),
            pltpu.VMEM((depth, patches, groups, group_rows, width), kind),
            pltpu.VMEM((steps, holders, groups, group_rows, width), kind),
            pltpu.VMEM((steps, lags, rows, unknowns), kind),
            pltpu.VMEM((lags, rows, unknowns), kind),
            pltpu.VMEM((steps, groups, lags, rows, unknowns), kind),
            pltpu.VMEM((steps, holders, groups, group_rows, width), kind),
            pltpu.VMEM((steps, patches, group_rows, width), kind),
            pltpu.VMEM((patches, group_rows, width), kind),
            pltpu.VMEM((steps - 1, min(lags, steps - 1), patches, group_rows, width), kind),
            pltpu.VMEM((lags, 1, patches), jnp.int32),
            pltpu.SMEM((lags, 1, patches), jnp.int32),
            dma, dma, dma, dma, dma, dma((depth,)), dma((steps,)),
            dma((steps,)), dma((steps,)), dma((steps,)), dma((steps,)), dma((steps, lags)),
            dma((3,)), dma, dma, dma,
        ],
        compiler_params=pltpu.CompilerParams(
            collective_id=0, has_side_effects=True, vmem_limit_bytes=48 * 1024 * 1024
        ),
    )(history.reshape(groups, group_rows, unknowns), coupling, inverse, cotangent, targets)


def solution(mesh):
    placed = (
        P("lag", None, "patch"),
        P("lag", "patch", None),
        P("patch", None),
        P(None, "lag", "patch"),
        P("lag", None),
    )
    return jax.shard_map(
        functools.partial(on_device, mesh.shape["patch"], mesh.shape["lag"]),
        mesh=mesh, in_specs=placed, out_specs=P(None, "lag", "patch"), check_vma=False,
    )
```
